512 devices in a mesh: row: 32 (over z, x), col: 16 (over y, core).
Axes of the slice: x: 4, y: 8, z: 8, core: 2. Of those that a mesh axis runs over, the one named last changes fastest.
Arguments:
- motion: bfloat16 [32768, 512], P(('row', 'col')), may hold values from -8 to 8
- text: bfloat16 [32768, 512], P(('row', 'col')), may hold values from -8 to 8
- pair_text: int32 [32768], P(('row', 'col')), may hold values from 0 to 32767, each once
Outputs:
- motion_grad: bfloat16 [32768, 512], P(('row', 'col'))
- text_grad: bfloat16 [32768, 512], P(('row', 'col'))
The draws below stay inside these ranges and needn't reach their ends.
Inputs may be any that keep to these rules, and one draw needn't show every extreme that they name: `pair_text`: every text row is the positive of exactly one motion row.
All inputs are finite; a program needn't handle non-finite values.
Results may differ from the reference program's by a relative error of at most 0.022.
Values may be sent and summed in bfloat16 or wider, within the bound.
No kernel may reach another device: no remote copies, remote signals or barrier semaphores. Data moves between devices by JAX's collectives and lax.ppermute only.
A program may use at most 64 MiB of HBM per device.

```python
import jax
import jax.numpy as jnp
from jax import lax

D = 512
PAIR_DEV = 64
PAIRS = 32768
N_ROW = 32
N_COL = 16


SIGMA = 0.095


def embedding_rows(key, low, high, twin):
    key = jax.random.fold_in(key, 101)
    k_normal = jax.random.fold_in(key, 0)
    k_scale = jax.random.fold_in(key, 2)
    normal_part = jax.random.truncated_normal(k_normal, -6.0, 6.0, (PAIRS, D), jnp.float32)
    base = normal_part
    scales = jnp.exp(jax.random.uniform(k_scale, (PAIRS, 1), jnp.float32, math_log(low), math_log(high)))
    rows = SIGMA * scales * base
    position = lax.broadcasted_iota(jnp.int32, (PAIRS, 1), 0)
    blend = twin * (position % 64 == 0).astype(jnp.float32)
    return (1.0 - blend) * rows


def math_log(value):
    return jnp.log(jnp.float32(value))


def draw_text(key, part):
    rows = embedding_rows(key, 0.6, 1.6, 0.0)
    return rows.astype(jnp.bfloat16)


def draw_motion(key, part):
    key = jax.random.fold_in(key, 7)
    rows = embedding_rows(key, 0.6, 1.6, 0.0)
    return rows.astype(jnp.bfloat16)


def setup_inputs(seed: int = 0) -> dict:
    streams_of = jax.random.split(jax.random.key(seed), 4)
    return {
        "motion": draw_motion(jax.random.fold_in(streams_of[3], 71), 0),
        "text": draw_text(jax.random.fold_in(streams_of[3], 71), 0),
        "pair_text": jax.random.permutation(streams_of[2], PAIRS).astype(jnp.int32),
    }


TAU = 0.1


def scores_of(rows, cols):
    return jnp.dot(rows.astype(jnp.float32), cols.astype(jnp.float32).T, precision=lax.Precision.HIGHEST) / TAU


def log_total(scores, axis):
    peak = jnp.max(scores, axis=axis, keepdims=True)
    return jnp.squeeze(peak, axis) + jnp.log(jnp.sum(jnp.exp(scores - peak), axis=axis))


def reference(motion, text, pair_text):
    block_rows = PAIR_DEV * N_COL
    block_cols = PAIR_DEV * N_ROW
    motion_blocks = motion.reshape(N_ROW, block_rows, D)
    text_blocks = text.reshape(N_ROW, N_COL, PAIR_DEV, D).transpose(1, 0, 2, 3).reshape(N_COL, block_cols, D)
    pair_blocks = pair_text.reshape(N_ROW, block_rows)
    row_lse = lax.map(lambda rows: log_total(scores_of(rows, text), 1), motion_blocks)
    col_lse = lax.map(lambda cols: log_total(scores_of(motion, cols), 0), text_blocks)
    col_index = jnp.arange(N_COL, dtype=jnp.int32)
    within = jnp.arange(block_cols, dtype=jnp.int32)

    def outer(text_total, row_items):
        rows, row_stat, pairs = row_items

        def inner(motion_total, col_items):
            cols, col_stat, index = col_items
            scores = scores_of(rows, cols)
            ids = (within // PAIR_DEV * N_COL + index) * PAIR_DEV + within % PAIR_DEV
            positive = (pairs[:, None] == ids[None, :]).astype(jnp.float32)
            weights = ((jnp.exp(scores - row_stat[:, None]) + jnp.exp(scores - col_stat[None, :]) - 2.0 * positive) / (2.0 * TAU)).astype(jnp.bfloat16)
            wide = weights.astype(jnp.float32)
            to_motion = jnp.dot(wide, cols.astype(jnp.float32), precision=lax.Precision.HIGHEST).astype(jnp.bfloat16)
            to_text = jnp.dot(wide.T, rows.astype(jnp.float32), precision=lax.Precision.HIGHEST).astype(jnp.bfloat16)
            to_motion = lax.optimization_barrier(to_motion)
            return motion_total + to_motion.astype(jnp.float32), to_text

        motion_total, to_text = lax.scan(inner, jnp.zeros((block_rows, D), jnp.float32), (text_blocks, col_lse, col_index))
        to_text = lax.optimization_barrier(to_text)
        return text_total + to_text.astype(jnp.float32), motion_total.astype(jnp.bfloat16)

    text_total, motion_grad = lax.scan(outer, jnp.zeros((N_COL, block_cols, D), jnp.float32), (motion_blocks, row_lse, pair_blocks))
    text_grad = text_total.astype(jnp.bfloat16).reshape(N_COL, N_ROW, PAIR_DEV, D).transpose(1, 0, 2, 3).reshape(PAIRS, D)
    return motion_grad.reshape(PAIRS, D), text_grad
```

```python
import jax
import jax.numpy as jnp
from jax import lax
from jax.sharding import Mesh, PartitionSpec as P

TAU = 0.1
AX = "d"
NZ, NX, NY, NC = 8, 4, 8, 2
DEVICES = NZ * NX * NY * NC


def dev(z, x, y, c):
    return ((z * NX + x) * NY + y) * NC + c


MOTION_PAIRS = ((0, 1), (2, 3))
TEXT_PAIRS = ((0, 3), (1, 2))
MOTION_GROUPS = [
    [dev(z, x, y, 1) for x in pair for y in range(NY)] for z in range(NZ) for pair in MOTION_PAIRS
]
TEXT_GROUPS = [
    [dev(z, x, y, 0) for x in pair for z in range(NZ)] for y in range(NY) for pair in TEXT_PAIRS
]
GROUPS = MOTION_GROUPS + TEXT_GROUPS
SWAP = [(i, i ^ 1) for i in range(DEVICES)]
TO_TEXT = [(i, i ^ 1) for i in range(1, DEVICES, 2)]
TO_MOTION = [(i, i ^ 1) for i in range(0, DEVICES, 2)]
G = 16


def swap(x):
    return lax.ppermute(x, AX, SWAP)


def exchange(x):
    return lax.all_to_all(x, AX, 0, 0, axis_index_groups=GROUPS)


def lse(x, axis):
    peak = jnp.max(x, axis=axis, keepdims=True)
    return jnp.squeeze(peak, axis) + jnp.log(jnp.sum(jnp.exp(x - peak), axis=axis))


def text_ids(d):
    chip = d // NC
    y = chip % NY
    x = chip // NY % NX
    n = lax.broadcasted_iota(jnp.int32, (1, G * 128), 1)
    k, rest = n // 128, n % 128
    outer = (x == 1) | (x == 2)
    xs = jnp.where(k < NZ, jnp.where(outer, 1, 0), jnp.where(outer, 2, 3))
    return (((k % NZ) * NX + xs) * NY + y) * 128 + rest


def per_device(motion, text, pair_text):
    n = motion.shape[0]
    d = lax.axis_index(AX)
    core = d % NC
    is_text = core == 0
    got = swap(jnp.where(is_text, motion, text))
    mine = jnp.where(is_text, jnp.concatenate([text, got]), jnp.concatenate([got, motion]))
    block = exchange(jnp.broadcast_to(mine[None], (G, 2 * n, mine.shape[1]))).reshape(G * 2 * n, -1)
    pair_got = swap(pair_text)
    other = swap(block)
    cols = jnp.where(is_text, block, other)
    rows = jnp.where(is_text, other[: G * n], block[G * n :])
    scores = (
        lax.dot_general(rows, cols, (((1,), (1,)), ((), ())), preferred_element_type=jnp.float32)
        / TAU
    )
    row_part = lse(scores, 1)
    col_part = lse(scores, 0)
    pad = jnp.zeros_like(row_part)
    stat_got = swap(jnp.where(is_text, jnp.concatenate([row_part, pad]), col_part))
    stat = jnp.where(
        is_text,
        jnp.logaddexp(col_part, stat_got),
        jnp.concatenate([stat_got[: G * n], row_part]),
    )
    pairs = jnp.concatenate([pair_got, pair_text]).astype(jnp.float32)
    stats = exchange(
        jnp.broadcast_to(jnp.concatenate([stat, pairs]).reshape(1, 17, 128), (G, 17, 128))
    )
    total = lse(stats[:, :16].reshape(G, 2048), 0)
    pair_all = stats[:, 16].reshape(2048)
    sent = jnp.where(is_text, total, jnp.concatenate([total[:1024], pair_all[:1024]]))
    total_got = swap(sent)
    col_lse = jnp.where(is_text, total, total_got)
    row_lse = jnp.where(is_text, total_got[:1024], total[1024:])
    pair_rows = jnp.where(is_text, total_got[1024:], pair_all[1024:]).astype(jnp.int32)
    positive = (pair_rows[:, None] == text_ids(d)).astype(jnp.float32)
    weights = (
        (jnp.exp(scores - row_lse[:, None]) + jnp.exp(scores - col_lse[None, :]) - 2.0 * positive)
        / (2.0 * TAU)
    ).astype(jnp.bfloat16)
    text_part = lax.dot_general(
        weights, rows, (((0,), (0,)), ((), ())), preferred_element_type=jnp.float32
    )
    motion_part = jnp.dot(weights, cols, preferred_element_type=jnp.float32).astype(jnp.bfloat16)
    text_got = lax.ppermute(text_part.astype(jnp.bfloat16), AX, TO_TEXT)
    motion_got = lax.ppermute(motion_part, AX, TO_MOTION)
    part = jnp.where(
        is_text,
        (text_part + text_got.astype(jnp.float32)).astype(jnp.bfloat16),
        jnp.concatenate([motion_got, motion_part]),
    )
    grads = exchange(part.reshape(G, 2 * n, -1))
    grad = jnp.sum(grads.astype(jnp.float32), axis=0).astype(jnp.bfloat16)
    grad_got = swap(jnp.where(is_text, grad[n:], grad[:n]))
    motion_grad = jnp.where(is_text, grad_got, grad[n:])
    text_grad = jnp.where(is_text, grad[:n], grad_got)
    return (motion_grad, text_grad)


def solution(mesh):
    flat = Mesh(mesh.devices.reshape(DEVICES), (AX,))
    return jax.shard_map(
        per_device,
        mesh=flat,
        in_specs=(P(AX, None), P(AX, None), P(AX)),
        out_specs=(P(AX, None), P(AX, None)),
        check_vma=False,
    )
```

```python
import jax
import jax.numpy as jnp
from jax import lax
from jax.sharding import Mesh, PartitionSpec as P

TAU = 0.1
AX = "d"
NZ, NX, NY, NC = 8, 4, 8, 2
DEVICES = NZ * NX * NY * NC


def dev(z, x, y, c):
    return ((z * NX + x) * NY + y) * NC + c


PAIRS_M = ((0, 1), (2, 3))
PAIRS_T = ((0, 3), (1, 2))
ZS, XS, YS, CS = range(NZ), range(NX), range(NY), range(NC)
RING_Y = [[dev(z, x, y, c) for y in YS] for z in ZS for x in XS for c in CS]
RING_Z = [[dev(z, x, y, c) for z in ZS] for y in YS for x in XS for c in CS]
GROUP_M = [[dev(z, x, y, c) for x in p for y in YS] for z in ZS for p in PAIRS_M for c in CS]
GROUP_T = [[dev(z, x, y, c) for x in p for z in ZS] for y in YS for p in PAIRS_T for c in CS]
SWAP_C = [(i, i ^ 1) for i in range(DEVICES)]
SWAP_M = [
    (dev(z, x, y, c), dev(z, x ^ 1, y, c)) for z in ZS for x in XS for y in YS for c in CS
]
SWAP_T = [
    (dev(z, x, y, c), dev(z, 3 - x, y, c)) for z in ZS for x in XS for y in YS for c in CS
]


def swap(x, pairs):
    return lax.ppermute(x, AX, pairs)


def exchange(x, groups):
    return lax.all_to_all(x, AX, 0, 0, axis_index_groups=groups)


def spread(x, groups):
    return exchange(jnp.broadcast_to(x[None], (len(groups[0]), *x.shape)), groups)


def lse(x, axis):
    peak = jnp.max(x, axis=axis, keepdims=True)
    return jnp.squeeze(peak, axis) + jnp.log(jnp.sum(jnp.exp(x - peak), axis=axis))


def dot(a, b, dims):
    return lax.dot_general(a, b, (dims, ((), ())), preferred_element_type=jnp.float32)


def text_ids(x, y, core, n):
    shape = (NZ, 2, n)
    z = lax.broadcasted_iota(jnp.int32, shape, 0)
    xs = jnp.where(lax.broadcasted_iota(jnp.int32, shape, 1) == 0, x, 3 - x)
    k = lax.broadcasted_iota(jnp.int32, shape, 2)
    return ((((z * NX + xs) * NY + y) * NC + core) * n + k).reshape(1, -1)


def per_device(motion, text, pair_text):
    n, width = motion.shape
    d = lax.axis_index(AX)
    core, y, x = d % NC, d // NC % NY, d // (NC * NY) % NX
    second_m, second_t = x % 2 == 1, x >= 2

    def order_m(v):
        v = v.reshape(2, -1)
        return jnp.where(second_m, v[::-1], v).reshape(-1)

    def order_t(v):
        v = v.reshape(NZ, 2, -1)
        return jnp.where(second_t, v[:, ::-1], v).reshape(-1)

    text_pair = jnp.concatenate([text, swap(text, SWAP_T)])
    rows_own = spread(motion, RING_Y).reshape(NY * n, width)
    rows = jnp.concatenate([rows_own, swap(rows_own, SWAP_M)])
    cols_own = spread(text_pair, RING_Z).reshape(NZ * 2 * n, width)
    cols_sib = swap(cols_own, SWAP_C)
    half = NZ * 2 * n

    s_own = dot(rows, cols_own, ((1,), (1,))) / TAU
    s_sib = dot(rows, cols_sib, ((1,), (1,))) / TAU
    col_own, col_sib = lse(s_own, 0), lse(s_sib, 0)
    col_part = jnp.logaddexp(col_own, swap(col_sib, SWAP_C))
    col_lse = lse(spread(order_t(col_part).reshape(-1, 128), GROUP_T), 0).reshape(-1)
    col_lse = order_t(col_lse)
    col_lse_sib = swap(col_lse, SWAP_C)
    row_peak = jnp.maximum(jnp.max(s_own, axis=1), jnp.max(s_sib, axis=1))
    row_sum = jnp.sum(jnp.exp(s_own - row_peak[:, None]), axis=1) + jnp.sum(
        jnp.exp(s_sib - row_peak[:, None]), axis=1
    )
    row_part = order_m(row_peak + jnp.log(row_sum))
    pairs = jnp.concatenate([pair_text.astype(jnp.float32), jnp.zeros((128 - n,), jnp.float32)])
    stats = spread(jnp.concatenate([row_part, pairs]).reshape(-1, 128), GROUP_M)
    row_lse = order_m(lse(stats[:, :-1], 0).reshape(-1))
    pair_rows = order_m(stats[:, -1, :n].reshape(-1)).astype(jnp.int32)

    def weights_of(scores, stat, ids):
        positive = (pair_rows[:, None] == ids).astype(jnp.float32)
        return (
            (jnp.exp(scores - row_lse[:, None]) + jnp.exp(scores - stat[None, :]) - 2.0 * positive)
            / (2.0 * TAU)
        ).astype(jnp.bfloat16)

    w_own = weights_of(s_own, col_lse, text_ids(x, y, core, n))
    w_sib = weights_of(s_sib, col_lse_sib, text_ids(x, y, 1 - core, n))
    text_sib = swap(dot(w_sib, rows, ((0,), (0,))).astype(jnp.bfloat16), SWAP_C)
    motion_part = dot(w_own, cols_own, ((1,), (0,))) + dot(w_sib, cols_sib, ((1,), (0,)))
    motion_part = motion_part.astype(jnp.bfloat16).reshape(2, NY, n, width).transpose(1, 0, 2, 3)
    motion_sum = jnp.sum(exchange(motion_part, RING_Y).astype(jnp.float32), axis=0)
    motion_got = swap(motion_sum[1].astype(jnp.bfloat16), SWAP_M)
    motion_grad = (motion_sum[0] + motion_got.astype(jnp.float32)).astype(jnp.bfloat16)

    text_part = dot(w_own, rows, ((0,), (0,))) + text_sib.astype(jnp.float32)
    text_part = text_part.reshape(NZ, 2, n, width)
    text_got = swap(text_part[:, 1].astype(jnp.bfloat16), SWAP_T)
    text_part = (text_part[:, 0] + text_got.astype(jnp.float32)).astype(jnp.bfloat16)
    text_sum = jnp.sum(exchange(text_part, RING_Z).astype(jnp.float32), axis=0)
    return (motion_grad, text_sum.astype(jnp.bfloat16))


def solution(mesh):
    flat = Mesh(mesh.devices.reshape(DEVICES), (AX,))
    return jax.shard_map(
        per_device,
        mesh=flat,
        in_specs=(P(AX, None), P(AX, None), P(AX)),
        out_specs=(P(AX, None), P(AX, None)),
        check_vma=False,
    )
```

```python
import functools
import math

import jax
import jax.numpy as jnp
from jax import lax
from jax.experimental import pallas as pl
from jax.experimental.pallas import tpu as pltpu
from jax.sharding import Mesh, PartitionSpec as P

TAU = 0.1
SCALE = math.log2(math.e) / TAU
AX = "d"
NZ, NX, NY, NC = 8, 4, 8, 2
DEVICES = NZ * NX * NY * NC
G = 16
LANES = 128


def dev(z, x, y, c):
    return ((z * NX + x) * NY + y) * NC + c


MOTION_GROUPS = [
    [dev(z, x, y, 1) for x in pair for y in range(NY)]
    for z in range(NZ)
    for pair in ((0, 1), (2, 3))
]
TEXT_GROUPS = [
    [dev(z, x, y, 0) for x in pair for z in range(NZ)]
    for y in range(NY)
    for pair in ((0, 3), (1, 2))
]
GROUPS = MOTION_GROUPS + TEXT_GROUPS
CORES = [(i, i ^ 1) for i in range(DEVICES)]


def swap(x):
    return lax.ppermute(x, AX, CORES)


def exchange(x):
    return lax.all_to_all(x, AX, 0, 0, axis_index_groups=GROUPS)


def spread(x):
    return exchange(jnp.broadcast_to(x[None], (G, *x.shape)))


def dot(a, b, dims):
    return lax.dot_general(a, b, (dims, ((), ())), preferred_element_type=jnp.float32)


def stats_kernel(chunks, x_ref, y_ref, out_ref):
    x = x_ref[...]
    n = y_ref.shape[0] // chunks
    peaks, sums = [], []
    for c in range(chunks):
        s = dot(y_ref[c * n : (c + 1) * n, :], x, ((1,), (1,))) * SCALE
        peak = jnp.max(s, axis=0, keepdims=True)
        peaks.append(peak)
        sums.append(jnp.sum(jnp.exp2(s - peak), axis=0, keepdims=True))
    peak = functools.reduce(jnp.maximum, peaks)
    total = sum(jnp.exp2(a - peak) * b for a, b in zip(peaks, sums))
    out_ref[0] = peak + jnp.log2(total)


def block_stats(x, y, block=1024, chunks=8):
    rows, width = x.shape
    steps = rows // block
    out = pl.pallas_call(
        functools.partial(stats_kernel, chunks),
        grid=(steps,),
        in_specs=[
            pl.BlockSpec((block, width), lambda i: (i, 0)),
            pl.BlockSpec(y.shape, lambda i: (0, 0)),
        ],
        out_specs=pl.BlockSpec((1, 1, block), lambda i: (i, 0, 0)),
        out_shape=jax.ShapeDtypeStruct((steps, 1, block), jnp.float32),
        compiler_params=pltpu.CompilerParams(vmem_limit_bytes=40 << 20),
        name="block_stats",
    )(x, y)
    return out.reshape(rows // LANES, LANES)


def columns(ref, first, count):
    return jnp.concatenate(
        [
            jnp.transpose(jnp.broadcast_to(ref[pl.ds(first + r, 1), :], (LANES, LANES)))
            for r in range(count)
        ]
    )


def grads_kernel(x_ref, y_ref, lx_ref, kx_ref, ly_ref, ky_ref, out_ref):
    count = x_ref.shape[0] // LANES
    first = pl.program_id(0) * count
    lx, kx = columns(lx_ref, first, count), columns(kx_ref, first, count)
    y = y_ref[...]
    scores = dot(x_ref[...], y, ((1,), (1,)))
    weights = []
    for r in range(y.shape[0] // LANES):
        s = scores[:, r * LANES : (r + 1) * LANES] * SCALE
        w = jnp.exp2(s - lx) + jnp.exp2(s - ly_ref[r : r + 1, :])
        w = jnp.where(kx == ky_ref[r : r + 1, :], w - 2.0, w) * (0.5 / TAU)
        weights.append(w.astype(jnp.bfloat16))
    out_ref[...] = dot(jnp.concatenate(weights, axis=1), y, ((1,), (0,))).astype(jnp.bfloat16)


def block_grads(x, y, lx, kx, ly, ky, block=1024):
    rows, width = x.shape
    whole = pl.BlockSpec((rows // LANES, LANES), lambda i: (0, 0))
    return pl.pallas_call(
        grads_kernel,
        grid=(rows // block,),
        in_specs=[
            pl.BlockSpec((block, width), lambda i: (i, 0)),
            pl.BlockSpec(y.shape, lambda i: (0, 0)),
            whole,
            whole,
            whole,
            whole,
        ],
        out_specs=pl.BlockSpec((block, width), lambda i: (i, 0)),
        out_shape=jax.ShapeDtypeStruct(x.shape, jnp.bfloat16),
        compiler_params=pltpu.CompilerParams(vmem_limit_bytes=40 << 20),
        name="block_grads",
    )(x, y, lx, kx, ly, ky)


def per_device(motion, text, pair_text):
    n, width = motion.shape
    d = lax.axis_index(AX)
    is_text = d % NC == 0
    got = swap(jnp.where(is_text, motion, text))
    mine = jnp.where(is_text, jnp.concatenate([text, got]), jnp.concatenate([got, motion]))
    x = spread(mine).reshape(G * NC * n, width)
    y = swap(x)
    pair_got = swap(pair_text)
    ids = d // NC * (NC * n) + lax.iota(jnp.int32, NC * n)
    key = jnp.where(is_text, ids, jnp.concatenate([pair_got, pair_text])).astype(jnp.float32)
    part = block_stats(x, y)
    stats = spread(jnp.concatenate([part, key[None]]))
    parts, kx = stats[:, :G], stats[:, G]
    peak = jnp.max(parts, axis=0)
    lx = peak + jnp.log2(jnp.sum(jnp.exp2(parts - peak), axis=0))
    other = swap(jnp.concatenate([lx, kx]))
    grad_part = block_grads(x, y, lx, kx, other[:G], other[G:])
    grads = exchange(grad_part.reshape(G, NC * n, width))
    grad = jnp.sum(grads.astype(jnp.float32), axis=0).astype(jnp.bfloat16)
    grad_got = swap(jnp.where(is_text, grad[n:], grad[:n]))
    motion_grad = jnp.where(is_text, grad_got, grad[n:])
    text_grad = jnp.where(is_text, grad[:n], grad_got)
    return (motion_grad, text_grad)


def solution(mesh):
    flat = Mesh(mesh.devices.reshape(DEVICES), (AX,))
    return jax.shard_map(
        per_device,
        mesh=flat,
        in_specs=(P(AX, None), P(AX, None), P(AX)),
        out_specs=(P(AX, None), P(AX, None)),
        check_vma=False,
    )
```

```python
import functools
import math

import jax
import jax.numpy as jnp
from jax import lax
from jax.experimental import pallas as pl
from jax.experimental.pallas import tpu as pltpu
from jax.sharding import Mesh, PartitionSpec as P

TAU = 0.1
SCALE = math.log2(math.e) / TAU
AX = "d"
NZ, NX, NY, NC = 8, 4, 8, 2
DEVICES = NZ * NX * NY * NC
G = 16
LANES = 128


def dev(z, x, y, c):
    return ((z * NX + x) * NY + y) * NC + c


MOTION_GROUPS = [
    [dev(z, x, y, 1) for x in pair for y in range(NY)]
    for z in range(NZ)
    for pair in ((0, 1), (2, 3))
]
TEXT_GROUPS = [
    [dev(z, x, y, 0) for x in pair for z in range(NZ)]
    for y in range(NY)
    for pair in ((0, 3), (1, 2))
]
GROUPS = MOTION_GROUPS + TEXT_GROUPS
CORES = [(i, i ^ 1) for i in range(DEVICES)]


def swap(x):
    return lax.ppermute(x, AX, CORES)


def exchange(x):
    return lax.all_to_all(x, AX, 0, 0, axis_index_groups=GROUPS)


def spread(x):
    return exchange(jnp.broadcast_to(x[None], (G, *x.shape)))


def dot(a, b, dims):
    return lax.dot_general(a, b, (dims, ((), ())), preferred_element_type=jnp.float32)


def stats_kernel(chunks, x_ref, y_ref, out_ref):
    x = x_ref[...]
    n = y_ref.shape[0] // chunks
    peaks, sums = [], []
    for c in range(chunks):
        s = dot(y_ref[c * n : (c + 1) * n, :], x, ((1,), (1,))) * SCALE
        peak = jnp.max(s, axis=0, keepdims=True)
        peaks.append(peak)
        sums.append(jnp.sum(jnp.exp2(s - peak), axis=0, keepdims=True))
    peak = functools.reduce(jnp.maximum, peaks)
    total = sum(jnp.exp2(a - peak) * b for a, b in zip(peaks, sums))
    out_ref[0] = peak + jnp.log2(total)


def block_stats(x, y, block=1024, chunks=8):
    rows, width = x.shape
    steps = rows // block
    out = pl.pallas_call(
        functools.partial(stats_kernel, chunks),
        grid=(steps,),
        in_specs=[
            pl.BlockSpec((block, width), lambda i: (i, 0)),
            pl.BlockSpec(memory_space=pltpu.VMEM),
        ],
        out_specs=pl.BlockSpec((1, 1, block), lambda i: (i, 0, 0)),
        out_shape=jax.ShapeDtypeStruct((steps, 1, block), jnp.float32),
        compiler_params=pltpu.CompilerParams(vmem_limit_bytes=40 << 20),
        name="block_stats",
    )(x, y)
    return out.reshape(rows // LANES, LANES)


def columns(ref, first, count):
    return jnp.concatenate(
        [
            jnp.transpose(jnp.broadcast_to(ref[pl.ds(first + r, 1), :], (LANES, LANES)))
            for r in range(count)
        ]
    )


VMEM = pl.BlockSpec(memory_space=pltpu.VMEM)


def scores_kernel(block, x_ref, y_ref, out_ref):
    y = y_ref[...]
    for i in range(0, x_ref.shape[0], block):
        out_ref[i : i + block, :] = dot(x_ref[i : i + block, :], y, ((1,), (1,))) * SCALE


def block_scores(x, y, block=512):
    rows, width = x.shape
    return pl.pallas_call(
        functools.partial(scores_kernel, block),
        in_specs=[VMEM, VMEM],
        out_specs=VMEM,
        out_shape=pltpu.VMEM((rows, y.shape[0]), jnp.float32),
        compiler_params=pltpu.CompilerParams(vmem_limit_bytes=20 << 20),
        cost_estimate=pl.CostEstimate(
            flops=2 * rows * y.shape[0] * width,
            bytes_accessed=4 * rows * y.shape[0] + 4 * rows * width,
            transcendentals=0,
        ),
        name="block_scores",
    )(x, y)


def grads_kernel(s_ref, y_ref, lx_ref, kx_ref, ly_ref, ky_ref, out_ref):
    block = out_ref.shape[0]
    count = block // LANES
    step = pl.program_id(0)
    lx, kx = columns(lx_ref, step * count, count), columns(kx_ref, step * count, count)
    rows = pl.ds(pl.multiple_of(step * block, block), block)
    weights = []
    for r in range(s_ref.shape[1] // LANES):
        s = s_ref[rows, r * LANES : (r + 1) * LANES]
        w = jnp.exp2(s - lx) + jnp.exp2(s - ly_ref[r : r + 1, :])
        w = jnp.where(kx == ky_ref[r : r + 1, :], w - 2.0, w) * (0.5 / TAU)
        weights.append(w.astype(jnp.bfloat16))
    w = jnp.concatenate(weights, axis=1)
    out_ref[...] = dot(w, y_ref[...], ((1,), (0,))).astype(jnp.bfloat16)


def block_grads(scores, y, lx, kx, ly, ky, block=1024):
    rows = scores.shape[0]
    width = y.shape[1]
    whole = pl.BlockSpec((rows // LANES, LANES), lambda i: (0, 0))
    return pl.pallas_call(
        grads_kernel,
        grid=(rows // block,),
        in_specs=[
            VMEM,
            VMEM,
            whole,
            whole,
            whole,
            whole,
        ],
        out_specs=pl.BlockSpec((block, width), lambda i: (i, 0)),
        out_shape=jax.ShapeDtypeStruct((rows, width), jnp.bfloat16),
        compiler_params=pltpu.CompilerParams(vmem_limit_bytes=28 << 20),
        name="block_grads",
    )(scores, y, lx, kx, ly, ky)


def per_device(motion, text, pair_text):
    n, width = motion.shape
    d = lax.axis_index(AX)
    is_text = d % NC == 0
    got = swap(jnp.where(is_text, motion, text))
    mine = jnp.where(is_text, jnp.concatenate([text, got]), jnp.concatenate([got, motion]))
    x = spread(mine).reshape(G * NC * n, width)
    y = swap(x)
    pair_got = swap(pair_text)
    ids = d // NC * (NC * n) + lax.iota(jnp.int32, NC * n)
    key = jnp.where(is_text, ids, jnp.concatenate([pair_got, pair_text])).astype(jnp.float32)
    part = block_stats(x, y)
    stats = spread(jnp.concatenate([part, key[None]]))
    parts, kx = stats[:, :G], stats[:, G]
    peak = jnp.max(parts, axis=0)
    lx = peak + jnp.log2(jnp.sum(jnp.exp2(parts - peak), axis=0))
    other = swap(jnp.concatenate([lx, kx]))
    grad_part = block_grads(block_scores(x, y), y, lx, kx, other[:G], other[G:])
    grads = exchange(grad_part.reshape(G, NC * n, width))
    grad = jnp.sum(grads.astype(jnp.float32), axis=0).astype(jnp.bfloat16)
    grad_got = swap(grad)
    motion_grad = jnp.where(is_text, grad_got[:n], grad[n:])
    text_grad = jnp.where(is_text, grad[:n], grad_got[n:])
    return (motion_grad, text_grad)


def solution(mesh):
    flat = Mesh(mesh.devices.reshape(DEVICES), (AX,))
    return jax.shard_map(
        per_device,
        mesh=flat,
        in_specs=(P(AX, None), P(AX, None), P(AX)),
        out_specs=(P(AX, None), P(AX, None)),
        check_vma=False,
    )
```

```python
import functools
import math

import jax
import jax.numpy as jnp
from jax import lax
from jax.experimental import pallas as pl
from jax.experimental.pallas import tpu as pltpu
from jax.sharding import Mesh, PartitionSpec as P

TAU = 0.1
SCALE = math.log2(math.e) / TAU
AX = "d"
NZ, NX, NY, NC = 8, 4, 8, 2
DEVICES = NZ * NX * NY * NC
G = 16
LANES = 128


def dev(z, x, y, c):
    return ((z * NX + x) * NY + y) * NC + c


MOTION_GROUPS = [
    [dev(z, x, y, 1) for x in pair for y in range(NY)]
    for z in range(NZ)
    for pair in ((0, 1), (2, 3))
]
TEXT_GROUPS = [
    [dev(z, x, y, 0) for x in pair for z in range(NZ)]
    for y in range(NY)
    for pair in ((0, 3), (1, 2))
]
GROUPS = MOTION_GROUPS + TEXT_GROUPS
CORES = [(i, i ^ 1) for i in range(DEVICES)]


def swap(x):
    return lax.ppermute(x, AX, CORES)


def exchange(x):
    return lax.all_to_all(x, AX, 0, 0, axis_index_groups=GROUPS)


def spread(x):
    return exchange(jnp.broadcast_to(x[None], (G, *x.shape)))


def dot(a, b, dims):
    return lax.dot_general(a, b, (dims, ((), ())), preferred_element_type=jnp.float32)


VMEM = pl.BlockSpec(memory_space=pltpu.VMEM)


def stats_kernel(chunks, x_ref, y_ref, out_ref, s_ref):
    x = x_ref[...]
    block = x.shape[0]
    rows = pl.ds(pl.multiple_of(pl.program_id(0) * block, block), block)
    n = y_ref.shape[0] // chunks
    peaks, sums = [], []
    for c in range(chunks):
        s = dot(x, y_ref[c * n : (c + 1) * n, :], ((1,), (1,))) * SCALE
        s_ref[rows, c * n : (c + 1) * n] = s
        peak = jnp.max(s, axis=1, keepdims=True)
        peaks.append(peak)
        sums.append(jnp.sum(jnp.exp2(s - peak), axis=1, keepdims=True))
    peak = functools.reduce(jnp.maximum, peaks)
    total = sum(jnp.exp2(a - peak) * b for a, b in zip(peaks, sums))
    v = peak + jnp.log2(total)
    for r in range(block // LANES):
        column = v[r * LANES : (r + 1) * LANES]
        out_ref[0, r : r + 1, :] = jnp.transpose(jnp.broadcast_to(column, (LANES, LANES)))[:1]


def block_stats(x, y, block=512, chunks=4):
    rows, width = x.shape
    steps = rows // block
    out, scores = pl.pallas_call(
        functools.partial(stats_kernel, chunks),
        grid=(steps,),
        in_specs=[pl.BlockSpec((block, width), lambda i: (i, 0)), VMEM],
        out_specs=[pl.BlockSpec((1, block // LANES, LANES), lambda i: (i, 0, 0)), VMEM],
        out_shape=[
            jax.ShapeDtypeStruct((steps, block // LANES, LANES), jnp.float32),
            pltpu.VMEM((rows, y.shape[0]), jnp.float32),
        ],
        compiler_params=pltpu.CompilerParams(vmem_limit_bytes=20 << 20),
        name="block_stats",
    )(x, y)
    return out.reshape(rows // LANES, LANES), scores


def combine_kernel(stats_ref, out_ref):
    parts = stats_ref[:, :G, :]
    peak = jnp.max(parts, axis=0)
    out_ref[:G, :] = peak + jnp.log2(jnp.sum(jnp.exp2(parts - peak), axis=0))
    out_ref[G:, :] = jnp.concatenate([stats_ref[g, G:, :] for g in range(G)])


def combine(stats):
    return pl.pallas_call(
        combine_kernel,
        in_specs=[VMEM],
        out_specs=VMEM,
        out_shape=jax.ShapeDtypeStruct((2 * G, LANES), jnp.float32),
        compiler_params=pltpu.CompilerParams(vmem_limit_bytes=4 << 20),
        name="combine",
    )(stats)


def columns(ref, first, count):
    return jnp.concatenate(
        [
            jnp.transpose(jnp.broadcast_to(ref[pl.ds(first + r, 1), :], (LANES, LANES)))
            for r in range(count)
        ]
    )


def grads_kernel(s_ref, y_ref, own_ref, other_ref, out_ref):
    block = out_ref.shape[0]
    count = block // LANES
    step = pl.program_id(0)
    lx = columns(own_ref, step * count, count)
    kx = columns(own_ref, G + step * count, count)
    rows = pl.ds(pl.multiple_of(step * block, block), block)
    weights = []
    for r in range(s_ref.shape[1] // LANES):
        s = s_ref[rows, r * LANES : (r + 1) * LANES]
        w = jnp.exp2(s - lx) + jnp.exp2(s - other_ref[r : r + 1, :])
        w = jnp.where(kx == other_ref[G + r : G + r + 1, :], w - 2.0, w) * (0.5 / TAU)
        weights.append(w.astype(jnp.bfloat16))
    w = jnp.concatenate(weights, axis=1)
    out_ref[...] = dot(w, y_ref[...], ((1,), (0,))).astype(jnp.bfloat16)


def block_grads(scores, y, own, other, block=1024):
    rows = scores.shape[0]
    width = y.shape[1]
    return pl.pallas_call(
        grads_kernel,
        grid=(rows // block,),
        in_specs=[VMEM, VMEM, VMEM, VMEM],
        out_specs=pl.BlockSpec((block, width), lambda i: (i, 0)),
        out_shape=jax.ShapeDtypeStruct((rows, width), jnp.bfloat16),
        compiler_params=pltpu.CompilerParams(vmem_limit_bytes=28 << 20),
        name="block_grads",
    )(scores, y, own, other)


def per_device(motion, text, pair_text):
    n, width = motion.shape
    d = lax.axis_index(AX)
    is_text = d % NC == 0
    got = swap(jnp.where(is_text, motion, text))
    mine = jnp.where(is_text, jnp.concatenate([text, got]), jnp.concatenate([got, motion]))
    x = spread(mine).reshape(G * NC * n, width)
    y = swap(x)
    pair_got = swap(pair_text)
    ids = d // NC * (NC * n) + lax.iota(jnp.int32, NC * n)
    key = jnp.where(is_text, ids, jnp.concatenate([pair_got, pair_text])).astype(jnp.float32)
    part, scores = block_stats(x, y)
    own = combine(spread(jnp.concatenate([part, key[None]])))
    grad_part = block_grads(scores, y, own, swap(own))
    grads = exchange(grad_part.reshape(G, NC * n, width))
    grad = jnp.sum(grads.astype(jnp.float32), axis=0).astype(jnp.bfloat16)
    grad_got = swap(grad)
    motion_grad = jnp.where(is_text, grad_got[:n], grad[n:])
    text_grad = jnp.where(is_text, grad[:n], grad_got[n:])
    return (motion_grad, text_grad)


def solution(mesh):
    flat = Mesh(mesh.devices.reshape(DEVICES), (AX,))
    return jax.shard_map(
        per_device,
        mesh=flat,
        in_specs=(P(AX, None), P(AX, None), P(AX)),
        out_specs=(P(AX, None), P(AX, None)),
        check_vma=False,
    )
```

```python
import functools
import math

import jax
import jax.numpy as jnp
from jax import lax
from jax.experimental import pallas as pl
from jax.experimental.pallas import tpu as pltpu
from jax.sharding import Mesh, PartitionSpec as P

TAU = 0.1
SCALE = math.log2(math.e) / TAU
FACTOR = math.log2(0.5 / TAU)
AX = "d"
NZ, NX, NY, NC = 8, 4, 8, 2
DEVICES = NZ * NX * NY * NC
G = 16
LANES = 128


def dev(z, x, y, c):
    return ((z * NX + x) * NY + y) * NC + c


MOTION_GROUPS = [
    [dev(z, x, y, 1) for x in pair for y in range(NY)]
    for z in range(NZ)
    for pair in ((0, 1), (2, 3))
]
TEXT_GROUPS = [
    [dev(z, x, y, 0) for x in pair for z in range(NZ)]
    for y in range(NY)
    for pair in ((0, 3), (1, 2))
]
GROUPS = MOTION_GROUPS + TEXT_GROUPS
CORES = [(i, i ^ 1) for i in range(DEVICES)]


def swap(x):
    return lax.ppermute(x, AX, CORES)


def exchange(x):
    return lax.all_to_all(x, AX, 0, 0, axis_index_groups=GROUPS)


def spread(x):
    return exchange(jnp.broadcast_to(x[None], (G, *x.shape)))


def dot(a, b, dims):
    return lax.dot_general(a, b, (dims, ((), ())), preferred_element_type=jnp.float32)


VMEM = pl.BlockSpec(memory_space=pltpu.VMEM)


def stats_kernel(chunks, x_ref, y_ref, out_ref, s_ref):
    x = x_ref[...]
    block = x.shape[0]
    rows = pl.ds(pl.multiple_of(pl.program_id(0) * block, block), block)
    n = y_ref.shape[0] // chunks
    peaks, sums = [], []
    for c in range(chunks):
        s = dot(x, y_ref[c * n : (c + 1) * n, :], ((1,), (1,))) * SCALE
        s_ref[rows, c * n : (c + 1) * n] = s
        peak = jnp.max(s, axis=1, keepdims=True)
        peaks.append(peak)
        sums.append(jnp.sum(jnp.exp2(s - peak), axis=1, keepdims=True))
    peak = functools.reduce(jnp.maximum, peaks)
    total = sum(jnp.exp2(a - peak) * b for a, b in zip(peaks, sums))
    v = peak + jnp.log2(total)
    for r in range(block // LANES):
        column = v[r * LANES : (r + 1) * LANES]
        out_ref[0, r : r + 1, :] = jnp.transpose(jnp.broadcast_to(column, (LANES, LANES)))[:1]


def block_stats(x, y, block=512, chunks=4):
    rows, width = x.shape
    steps = rows // block
    out, scores = pl.pallas_call(
        functools.partial(stats_kernel, chunks),
        grid=(steps,),
        in_specs=[pl.BlockSpec((block, width), lambda i: (i, 0)), VMEM],
        out_specs=[pl.BlockSpec((1, block // LANES, LANES), lambda i: (i, 0, 0)), VMEM],
        out_shape=[
            jax.ShapeDtypeStruct((steps, block // LANES, LANES), jnp.float32),
            pltpu.VMEM((rows, y.shape[0]), jnp.float32),
        ],
        compiler_params=pltpu.CompilerParams(vmem_limit_bytes=20 << 20),
        name="block_stats",
    )(x, y)
    return out.reshape(rows // LANES, LANES), scores


def combine_kernel(stats_ref, out_ref):
    parts = stats_ref[:, :G, :]
    peak = jnp.max(parts, axis=0)
    out_ref[:G, :] = (peak - FACTOR) + jnp.log2(jnp.sum(jnp.exp2(parts - peak), axis=0))
    out_ref[G:, :] = jnp.concatenate([stats_ref[g, G:, :] for g in range(G)])


def combine(stats):
    return pl.pallas_call(
        combine_kernel,
        in_specs=[VMEM],
        out_specs=VMEM,
        out_shape=jax.ShapeDtypeStruct((2 * G, LANES), jnp.float32),
        compiler_params=pltpu.CompilerParams(vmem_limit_bytes=4 << 20),
        name="combine",
    )(stats)


def columns(ref, first, count):
    return jnp.concatenate(
        [
            jnp.transpose(jnp.broadcast_to(ref[pl.ds(first + r, 1), :], (LANES, LANES)))
            for r in range(count)
        ]
    )


def grads_kernel(s_ref, y_ref, own_ref, other_ref, out_ref):
    block = out_ref.shape[0]
    count = block // LANES
    step = pl.program_id(0)
    lx = columns(own_ref, step * count, count)
    kx = columns(own_ref, G + step * count, count)
    rows = pl.ds(pl.multiple_of(step * block, block), block)
    weights = []
    for r in range(s_ref.shape[1] // LANES):
        s = s_ref[rows, r * LANES : (r + 1) * LANES]
        w = jnp.exp2(s - lx) + jnp.exp2(s - other_ref[r : r + 1, :])
        w = jnp.where(kx == other_ref[G + r : G + r + 1, :], w - 1.0 / TAU, w)
        weights.append(w.astype(jnp.bfloat16))
    w = jnp.concatenate(weights, axis=1)
    out_ref[...] = dot(w, y_ref[...], ((1,), (0,))).astype(jnp.bfloat16)


def block_grads(scores, y, own, other, block=1024):
    rows = scores.shape[0]
    width = y.shape[1]
    return pl.pallas_call(
        grads_kernel,
        grid=(rows // block,),
        in_specs=[VMEM, VMEM, VMEM, VMEM],
        out_specs=pl.BlockSpec((block, width), lambda i: (i, 0)),
        out_shape=jax.ShapeDtypeStruct((rows, width), jnp.bfloat16),
        compiler_params=pltpu.CompilerParams(vmem_limit_bytes=28 << 20),
        name="block_grads",
    )(scores, y, own, other)


def per_device(motion, text, pair_text):
    n, width = motion.shape
    d = lax.axis_index(AX)
    is_text = d % NC == 0
    got = swap(jnp.where(is_text, motion, text))
    mine = jnp.where(is_text, jnp.concatenate([text, got]), jnp.concatenate([got, motion]))
    x = spread(mine).reshape(G * NC * n, width)
    y = swap(x)
    pair_got = swap(pair_text)
    ids = d // NC * (NC * n) + lax.iota(jnp.int32, NC * n)
    key = jnp.where(is_text, ids, jnp.concatenate([pair_got, pair_text])).astype(jnp.float32)
    part, scores = block_stats(x, y)
    own = combine(spread(jnp.concatenate([part, key[None]])))
    grad_part = block_grads(scores, y, own, swap(own))
    grads = exchange(grad_part.reshape(G, NC * n, width))
    grad = jnp.sum(grads.astype(jnp.float32), axis=0).astype(jnp.bfloat16)
    grad_got = swap(grad)
    motion_grad = jnp.where(is_text, grad_got[:n], grad[n:])
    text_grad = jnp.where(is_text, grad[:n], grad_got[n:])
    return (motion_grad, text_grad)


def solution(mesh):
    flat = Mesh(mesh.devices.reshape(DEVICES), (AX,))
    return jax.shard_map(
        per_device,
        mesh=flat,
        in_specs=(P(AX, None), P(AX, None), P(AX)),
        out_specs=(P(AX, None), P(AX, None)),
        check_vma=False,
    )
```

```python
import functools
import math

import jax
import jax.numpy as jnp
from jax import lax
from jax.experimental import pallas as pl
from jax.experimental.pallas import tpu as pltpu
from jax.sharding import Mesh, PartitionSpec as P

TAU = 0.1
SCALE = math.log2(math.e) / TAU
FACTOR = math.log2(0.5 / TAU)
AX = "d"
NZ, NX, NY, NC = 8, 4, 8, 2
DEVICES = NZ * NX * NY * NC
G = 16
LANES = 128


def dev(z, x, y, c):
    return ((z * NX + x) * NY + y) * NC + c


MOTION_GROUPS = [
    [dev(z, x, y, 1) for x in pair for y in range(NY)]
    for z in range(NZ)
    for pair in ((0, 1), (2, 3))
]
TEXT_GROUPS = [
    [dev(z, x, y, 0) for x in pair for z in range(NZ)]
    for y in range(NY)
    for pair in ((0, 3), (1, 2))
]
GROUPS = MOTION_GROUPS + TEXT_GROUPS
CORES = [(i, i ^ 1) for i in range(DEVICES)]


def swap(x):
    return lax.ppermute(x, AX, CORES)


def exchange(x):
    return lax.all_to_all(x, AX, 0, 0, axis_index_groups=GROUPS)


def spread(x):
    return exchange(jnp.broadcast_to(x[None], (G, *x.shape)))


def dot(a, b, dims):
    return lax.dot_general(a, b, (dims, ((), ())), preferred_element_type=jnp.float32)


VMEM = pl.BlockSpec(memory_space=pltpu.VMEM)


def stats_kernel(chunks, x_ref, y_ref, out_ref, s_ref):
    x = x_ref[...]
    block = x.shape[0]
    rows = pl.ds(pl.multiple_of(pl.program_id(0) * block, block), block)
    n = y_ref.shape[0] // chunks
    peaks, sums = [], []
    for c in range(chunks):
        s = dot(x, y_ref[c * n : (c + 1) * n, :], ((1,), (1,))) * SCALE
        s_ref[rows, c * n : (c + 1) * n] = s
        peak = jnp.max(s, axis=1, keepdims=True)
        peaks.append(peak)
        sums.append(jnp.sum(jnp.exp2(s - peak), axis=1, keepdims=True))
    peak = functools.reduce(jnp.maximum, peaks)
    total = sum(jnp.exp2(a - peak) * b for a, b in zip(peaks, sums))
    v = peak + jnp.log2(total)
    for r in range(block // LANES):
        column = v[r * LANES : (r + 1) * LANES]
        out_ref[0, r : r + 1, :] = jnp.transpose(jnp.broadcast_to(column, (LANES, LANES)))[:1]


def block_stats(x, y, block=512, chunks=4):
    rows, width = x.shape
    steps = rows // block
    out, scores = pl.pallas_call(
        functools.partial(stats_kernel, chunks),
        grid=(steps,),
        in_specs=[pl.BlockSpec((block, width), lambda i: (i, 0)), VMEM],
        out_specs=[pl.BlockSpec((1, block // LANES, LANES), lambda i: (i, 0, 0)), VMEM],
        out_shape=[
            jax.ShapeDtypeStruct((steps, block // LANES, LANES), jnp.float32),
            pltpu.VMEM((rows, y.shape[0]), jnp.float32),
        ],
        compiler_params=pltpu.CompilerParams(vmem_limit_bytes=20 << 20),
        name="block_stats",
    )(x, y)
    return out.reshape(rows // LANES, LANES), scores


def combine_kernel(stats_ref, out_ref):
    parts = stats_ref[:, :G, :]
    peak = jnp.max(parts, axis=0)
    out_ref[:G, :] = (peak - FACTOR) + jnp.log2(jnp.sum(jnp.exp2(parts - peak), axis=0))
    out_ref[G:, :] = jnp.concatenate([stats_ref[g, G:, :] for g in range(G)])


def combine(stats):
    return pl.pallas_call(
        combine_kernel,
        in_specs=[VMEM],
        out_specs=VMEM,
        out_shape=jax.ShapeDtypeStruct((2 * G, LANES), jnp.float32),
        compiler_params=pltpu.CompilerParams(vmem_limit_bytes=4 << 20),
        name="combine",
    )(stats)


def columns(ref, first, count):
    return jnp.concatenate(
        [
            jnp.transpose(jnp.broadcast_to(ref[pl.ds(first + r, 1), :], (LANES, LANES)))
            for r in range(count)
        ]
    )


def grads_kernel(s_ref, y_ref, own_ref, other_ref, out_ref):
    block = out_ref.shape[0]
    count = block // LANES
    step = pl.program_id(0)
    lx = columns(own_ref, step * count, count)
    kx = columns(own_ref, G + step * count, count)
    rows = pl.ds(pl.multiple_of(step * block, block), block)
    weights = []
    for r in range(s_ref.shape[1] // LANES):
        s = s_ref[rows, r * LANES : (r + 1) * LANES]
        w = jnp.exp2(s - lx) + jnp.exp2(s - other_ref[r : r + 1, :])
        w = jnp.where(kx == other_ref[G + r : G + r + 1, :], w - 1.0 / TAU, w)
        weights.append(w.astype(jnp.bfloat16))
    w = jnp.concatenate(weights, axis=1)
    out_ref[...] = dot(w, y_ref[...], ((1,), (0,))).astype(jnp.bfloat16)


def block_grads(scores, y, own, other, block=1024):
    rows = scores.shape[0]
    width = y.shape[1]
    return pl.pallas_call(
        grads_kernel,
        grid=(rows // block,),
        in_specs=[VMEM, VMEM, VMEM, VMEM],
        out_specs=pl.BlockSpec((block, width), lambda i: (i, 0)),
        out_shape=jax.ShapeDtypeStruct((rows, width), jnp.bfloat16),
        compiler_params=pltpu.CompilerParams(vmem_limit_bytes=28 << 20),
        name="block_grads",
    )(scores, y, own, other)


def per_device(motion, text, pair_text):
    n, width = motion.shape
    d = lax.axis_index(AX)
    is_text = d % NC == 0
    shard = lax.optimization_barrier(jnp.where(is_text, text, motion))
    got = swap(jnp.where(is_text, motion, text))
    mine = jnp.where(is_text, jnp.concatenate([shard, got]), jnp.concatenate([got, shard]))
    x = spread(mine).reshape(G * NC * n, width)
    y = swap(x)
    pair_got = swap(pair_text)
    ids = d // NC * (NC * n) + lax.iota(jnp.int32, NC * n)
    key = jnp.where(is_text, ids, jnp.concatenate([pair_got, pair_text])).astype(jnp.float32)
    part, scores = block_stats(x, y)
    own = combine(spread(jnp.concatenate([part, key[None]])))
    grad_part = block_grads(scores, y, own, swap(own))
    grads = exchange(grad_part.reshape(G, NC * n, width))
    grad = jnp.sum(grads.astype(jnp.float32), axis=0).astype(jnp.bfloat16)
    grad_got = swap(grad)
    motion_grad = jnp.where(is_text, grad_got[:n], grad[n:])
    text_grad = jnp.where(is_text, grad[:n], grad_got[n:])
    return (motion_grad, text_grad)


def solution(mesh):
    flat = Mesh(mesh.devices.reshape(DEVICES), (AX,))
    return jax.shard_map(
        per_device,
        mesh=flat,
        in_specs=(P(AX, None), P(AX, None), P(AX)),
        out_specs=(P(AX, None), P(AX, None)),
        check_vma=False,
    )
```

```python
import functools
import math

import jax
import jax.numpy as jnp
from jax import lax
from jax.experimental import pallas as pl
from jax.experimental.pallas import tpu as pltpu
from jax.sharding import Mesh, PartitionSpec as P

TAU = 0.1
SCALE = math.log2(math.e) / TAU
FACTOR = math.log2(0.5 / TAU)
AX = "d"
NZ, NX, NY, NC = 8, 4, 8, 2
DEVICES = NZ * NX * NY * NC
G = 16
LANES = 128


def dev(z, x, y, c):
    return ((z * NX + x) * NY + y) * NC + c


MOTION_GROUPS = [
    [dev(z, x, y, 1) for x in pair for y in range(NY)]
    for z in range(NZ)
    for pair in ((0, 1), (2, 3))
]
TEXT_GROUPS = [
    [dev(z, x, y, 0) for x in pair for z in range(NZ)]
    for y in range(NY)
    for pair in ((0, 3), (1, 2))
]
GROUPS = MOTION_GROUPS + TEXT_GROUPS
CORES = [(i, i ^ 1) for i in range(DEVICES)]


def swap(x):
    return lax.ppermute(x, AX, CORES)


def exchange(x):
    return lax.all_to_all(x, AX, 0, 0, axis_index_groups=GROUPS)


def spread(x):
    return exchange(jnp.broadcast_to(x[None], (G, *x.shape)))


def dot(a, b, dims):
    return lax.dot_general(a, b, (dims, ((), ())), preferred_element_type=jnp.float32)


VMEM = pl.BlockSpec(memory_space=pltpu.VMEM)


def stats_kernel(chunks, x_ref, y_ref, out_ref, s_ref):
    x = x_ref[...]
    block = x.shape[0]
    rows = pl.ds(pl.multiple_of(pl.program_id(0) * block, block), block)
    n = y_ref.shape[0] // chunks
    peaks, sums = [], []
    for c in range(chunks):
        s = dot(x, y_ref[c * n : (c + 1) * n, :], ((1,), (1,))) * SCALE
        s_ref[rows, c * n : (c + 1) * n] = s
        peak = jnp.max(s, axis=1, keepdims=True)
        peaks.append(peak)
        sums.append(jnp.sum(jnp.exp2(s - peak), axis=1, keepdims=True))
    peak = functools.reduce(jnp.maximum, peaks)
    total = sum(jnp.exp2(a - peak) * b for a, b in zip(peaks, sums))
    v = peak + jnp.log2(total)
    for r in range(block // LANES):
        column = v[r * LANES : (r + 1) * LANES]
        out_ref[0, r : r + 1, :] = jnp.transpose(jnp.broadcast_to(column, (LANES, LANES)))[:1]


def block_stats(x, y, block=512, chunks=4):
    rows, width = x.shape
    steps = rows // block
    out, scores = pl.pallas_call(
        functools.partial(stats_kernel, chunks),
        grid=(steps,),
        in_specs=[pl.BlockSpec((block, width), lambda i: (i, 0)), VMEM],
        out_specs=[pl.BlockSpec((1, block // LANES, LANES), lambda i: (i, 0, 0)), VMEM],
        out_shape=[
            jax.ShapeDtypeStruct((steps, block // LANES, LANES), jnp.float32),
            pltpu.VMEM((rows, y.shape[0]), jnp.float32),
        ],
        compiler_params=pltpu.CompilerParams(vmem_limit_bytes=20 << 20),
        name="block_stats",
    )(x, y)
    return out.reshape(rows // LANES, LANES), scores


def combine_kernel(stats_ref, out_ref):
    parts = stats_ref[:, :G, :]
    peak = jnp.max(parts, axis=0)
    out_ref[:G, :] = (peak - FACTOR) + jnp.log2(jnp.sum(jnp.exp2(parts - peak), axis=0))
    out_ref[G:, :] = jnp.concatenate([stats_ref[g, G:, :] for g in range(G)])


def combine(stats):
    return pl.pallas_call(
        combine_kernel,
        in_specs=[VMEM],
        out_specs=VMEM,
        out_shape=jax.ShapeDtypeStruct((2 * G, LANES), jnp.float32),
        compiler_params=pltpu.CompilerParams(vmem_limit_bytes=4 << 20),
        name="combine",
    )(stats)


def columns(ref, first, count):
    return jnp.concatenate(
        [
            jnp.transpose(jnp.broadcast_to(ref[pl.ds(first + r, 1), :], (LANES, LANES)))
            for r in range(count)
        ]
    )


def grads_kernel(block, s_ref, y_ref, own_ref, other_ref, out_ref):
    count = block // LANES
    step = pl.program_id(0)
    lx = columns(own_ref, step * count, count)
    kx = columns(own_ref, G + step * count, count)
    rows = pl.ds(pl.multiple_of(step * block, block), block)
    weights = []
    for r in range(s_ref.shape[1] // LANES):
        s = s_ref[rows, r * LANES : (r + 1) * LANES]
        w = jnp.exp2(s - lx) + jnp.exp2(s - other_ref[r : r + 1, :])
        w = jnp.where(kx == other_ref[G + r : G + r + 1, :], w - 1.0 / TAU, w)
        weights.append(w.astype(jnp.bfloat16))
    w = jnp.concatenate(weights, axis=1)
    out_ref[rows, :] = dot(w, y_ref[...], ((1,), (0,))).astype(jnp.bfloat16)


def block_grads(scores, y, own, other, block=1024):
    rows = scores.shape[0]
    width = y.shape[1]
    return pl.pallas_call(
        functools.partial(grads_kernel, block),
        grid=(rows // block,),
        in_specs=[VMEM, VMEM, VMEM, VMEM],
        out_specs=VMEM,
        out_shape=jax.ShapeDtypeStruct((rows, width), jnp.bfloat16),
        compiler_params=pltpu.CompilerParams(vmem_limit_bytes=28 << 20),
        name="block_grads",
    )(scores, y, own, other)


def per_device(motion, text, pair_text):
    n, width = motion.shape
    d = lax.axis_index(AX)
    is_text = d % NC == 0
    shard = lax.optimization_barrier(jnp.where(is_text, text, motion))
    got = swap(jnp.where(is_text, motion, text))
    mine = jnp.where(is_text, jnp.concatenate([shard, got]), jnp.concatenate([got, shard]))
    x = spread(mine).reshape(G * NC * n, width)
    y = swap(x)
    pair_got = swap(pair_text)
    ids = d // NC * (NC * n) + lax.iota(jnp.int32, NC * n)
    key = jnp.where(is_text, ids, jnp.concatenate([pair_got, pair_text])).astype(jnp.float32)
    part, scores = block_stats(x, y)
    own = combine(spread(jnp.concatenate([part, key[None]])))
    grad_part = block_grads(scores, y, own, swap(own))
    grads = exchange(grad_part.reshape(G, NC * n, width))
    grad = jnp.sum(grads.astype(jnp.float32), axis=0).astype(jnp.bfloat16)
    grad_got = swap(grad)
    motion_grad = jnp.where(is_text, grad_got[:n], grad[n:])
    text_grad = jnp.where(is_text, grad[:n], grad_got[n:])
    return (motion_grad, text_grad)


def solution(mesh):
    flat = Mesh(mesh.devices.reshape(DEVICES), (AX,))
    return jax.shard_map(
        per_device,
        mesh=flat,
        in_specs=(P(AX, None), P(AX, None), P(AX)),
        out_specs=(P(AX, None), P(AX, None)),
        check_vma=False,
    )
```

```python
import functools
import math

import jax
import jax.numpy as jnp
from jax import lax
from jax.experimental import pallas as pl
from jax.experimental.pallas import tpu as pltpu
from jax.sharding import Mesh, PartitionSpec as P

TAU = 0.1
SCALE = math.log2(math.e) / TAU
FACTOR = math.log2(0.5 / TAU)
AX = "d"
NZ, NX, NY, NC = 8, 4, 8, 2
DEVICES = NZ * NX * NY * NC
G = 16
LANES = 128


def dev(z, x, y, c):
    return ((z * NX + x) * NY + y) * NC + c


MOTION_GROUPS = [
    [dev(z, x, y, 1) for x in pair for y in range(NY)]
    for z in range(NZ)
    for pair in ((0, 1), (2, 3))
]
TEXT_GROUPS = [
    [dev(z, x, y, 0) for x in pair for z in range(NZ)]
    for y in range(NY)
    for pair in ((0, 3), (1, 2))
]
GROUPS = MOTION_GROUPS + TEXT_GROUPS
CORES = [(i, i ^ 1) for i in range(DEVICES)]


def swap(x):
    return lax.ppermute(x, AX, CORES)


def exchange(x):
    return lax.all_to_all(x, AX, 0, 0, axis_index_groups=GROUPS)


def spread(x):
    return exchange(jnp.broadcast_to(x[None], (G, *x.shape)))


def dot(a, b, dims):
    return lax.dot_general(a, b, (dims, ((), ())), preferred_element_type=jnp.float32)


VMEM = pl.BlockSpec(memory_space=pltpu.VMEM)


def stats_kernel(chunks, x_ref, y_ref, out_ref, s_ref):
    x = x_ref[...]
    block = x.shape[0]
    rows = pl.ds(pl.multiple_of(pl.program_id(0) * block, block), block)
    n = y_ref.shape[0] // chunks
    peaks, sums = [], []
    for c in range(chunks):
        s = dot(x, y_ref[c * n : (c + 1) * n, :], ((1,), (1,))) * SCALE
        s_ref[rows, c * n : (c + 1) * n] = s
        peak = jnp.max(s, axis=1, keepdims=True)
        peaks.append(peak)
        sums.append(jnp.sum(jnp.exp2(s - peak), axis=1, keepdims=True))
    peak = functools.reduce(jnp.maximum, peaks)
    total = sum(jnp.exp2(a - peak) * b for a, b in zip(peaks, sums))
    v = peak + jnp.log2(total)
    for r in range(block // LANES):
        column = v[r * LANES : (r + 1) * LANES]
        out_ref[0, r : r + 1, :] = jnp.transpose(jnp.broadcast_to(column, (LANES, LANES)))[:1]


def block_stats(x, y, block=512, chunks=4):
    rows, width = x.shape
    steps = rows // block
    out, scores = pl.pallas_call(
        functools.partial(stats_kernel, chunks),
        grid=(steps,),
        in_specs=[pl.BlockSpec((block, width), lambda i: (i, 0)), VMEM],
        out_specs=[pl.BlockSpec((1, block // LANES, LANES), lambda i: (i, 0, 0)), VMEM],
        out_shape=[
            jax.ShapeDtypeStruct((steps, block // LANES, LANES), jnp.float32),
            pltpu.VMEM((rows, y.shape[0]), jnp.float32),
        ],
        compiler_params=pltpu.CompilerParams(vmem_limit_bytes=20 << 20),
        name="block_stats",
    )(x, y)
    return out.reshape(rows // LANES, LANES), scores


def combine_kernel(stats_ref, out_ref):
    parts = stats_ref[:, :G, :]
    peak = jnp.max(parts, axis=0)
    out_ref[:G, :] = (peak - FACTOR) + jnp.log2(jnp.sum(jnp.exp2(parts - peak), axis=0))
    out_ref[G:, :] = jnp.concatenate([stats_ref[g, G:, :] for g in range(G)])


def combine(stats):
    return pl.pallas_call(
        combine_kernel,
        in_specs=[VMEM],
        out_specs=VMEM,
        out_shape=jax.ShapeDtypeStruct((2 * G, LANES), jnp.float32),
        compiler_params=pltpu.CompilerParams(vmem_limit_bytes=4 << 20),
        name="combine",
    )(stats)


def columns(ref, first, count):
    return jnp.concatenate(
        [
            jnp.transpose(jnp.broadcast_to(ref[pl.ds(first + r, 1), :], (LANES, LANES)))
            for r in range(count)
        ]
    )


def grads_kernel(block, s_ref, y_ref, own_ref, other_ref, out_ref):
    count = block // LANES
    step = pl.program_id(0)
    lx = columns(own_ref, step * count, count)
    kx = columns(own_ref, G + step * count, count)
    rows = pl.ds(pl.multiple_of(step * block, block), block)
    weights = []
    for r in range(s_ref.shape[1] // LANES):
        s = s_ref[rows, r * LANES : (r + 1) * LANES]
        w = jnp.exp2(s - lx) + jnp.exp2(s - other_ref[r : r + 1, :])
        w = jnp.where(kx == other_ref[G + r : G + r + 1, :], w - 1.0 / TAU, w)
        weights.append(w.astype(jnp.bfloat16))
    w = jnp.concatenate(weights, axis=1)
    out_ref[rows, :] = dot(w, y_ref[...], ((1,), (0,))).astype(jnp.bfloat16)


def block_grads(scores, y, own, other, block=1024):
    rows = scores.shape[0]
    width = y.shape[1]
    return pl.pallas_call(
        functools.partial(grads_kernel, block),
        grid=(rows // block,),
        in_specs=[VMEM, VMEM, VMEM, VMEM],
        out_specs=VMEM,
        out_shape=jax.ShapeDtypeStruct((rows, width), jnp.bfloat16),
        compiler_params=pltpu.CompilerParams(vmem_limit_bytes=28 << 20),
        name="block_grads",
    )(scores, y, own, other)


def per_device(motion, text, pair_text):
    n, width = motion.shape
    d = lax.axis_index(AX)
    is_text = d % NC == 0
    shard = lax.optimization_barrier(jnp.where(is_text, text, motion))
    got = swap(jnp.where(is_text, motion, text))
    mine = jnp.where(is_text, jnp.concatenate([shard, got]), jnp.concatenate([got, shard]))
    x = spread(mine).reshape(G * NC * n, width)
    y = swap(x)
    pair_got = swap(pair_text)
    ids = d // NC * (NC * n) + lax.iota(jnp.int32, NC * n)
    key = jnp.where(is_text, ids, jnp.concatenate([pair_got, pair_text])).astype(jnp.float32)
    part, scores = block_stats(x, y)
    own = combine(spread(jnp.concatenate([part, key[None]])))
    grad_part = block_grads(scores, y, own, swap(own))
    grads = exchange(grad_part.reshape(G, NC * n, width))
    grad = jnp.sum(grads.astype(jnp.float32), axis=0).astype(jnp.bfloat16)
    grad_got = swap(jnp.where(is_text, grad[n:], grad[:n]))
    motion_grad = jnp.where(is_text, grad_got, grad[n:])
    text_grad = jnp.where(is_text, grad[:n], grad_got)
    return (motion_grad, text_grad)


def solution(mesh):
    flat = Mesh(mesh.devices.reshape(DEVICES), (AX,))
    return jax.shard_map(
        per_device,
        mesh=flat,
        in_specs=(P(AX, None), P(AX, None), P(AX)),
        out_specs=(P(AX, None), P(AX, None)),
        check_vma=False,
    )
```
